32 devices in a mesh: groups: 2 (over x), dp: 16 (over z, y, core).
Axes of the slice: x: 2, y: 2, z: 4, core: 2. Of those that a mesh axis runs over, the one named last changes fastest.
Arguments:
- acts: bfloat16 [1792, 8192], P(('groups', 'dp')), parts along dimension 0, may hold values from -6 to 6
- out_grad: bfloat16 [1792, 8192], P(('groups', 'dp')), parts along dimension 0, may hold values from -6 to 6
- gate_factor: bfloat16 [1792, 28672], P(('groups', 'dp')), parts along dimension 0, may hold values from -4 to 4
- down_weight: bfloat16 [28672, 8192], P('dp'), may hold values from -0.03125 to 0.03125
- proj_in: bfloat16 [64, 8192], replicated, may hold values from -0.0625 to 0.0625
- proj_out: bfloat16 [64, 28672], P(None, 'dp'), may hold values from -0.03125 to 0.03125
- lengths: int32 [32, 4], P(('groups', 'dp')), parts along dimension 0, may hold values from 1 to 28, 56 in all within a row
- queries: float32 [2048, 4096], P('dp'), may hold values from -4 to 4
Outputs:
- scores: float32 [128, 2048], P('groups', 'dp'), parts along dimension 0
The draws below stay inside these ranges and needn't reach their ends.
There are 2 independent parts, one for each index of `groups`. The reference program is written for one: setup_inputs(seed, part) draws one part's arguments, and reference() takes and returns one part's arrays. A program takes and returns all parts, laid end to end along the dimension named above; an argument that names none is the same for every part. Nothing has to cross between parts.
Inputs may be any that keep to these rules, and one draw needn't show every extreme that they name: `lengths`: each row lists the token counts of the 4 examples of one block of 56 tokens, in order; each row sums to 56.
All inputs are finite; a program needn't handle non-finite values.
Results may differ from the reference program's by a relative error of at most 0.003.
Values may be sent and summed in bfloat16 or wider, within the bound.
No kernel may reach another device: no remote copies, remote signals or barrier semaphores. Data moves between devices by JAX's collectives and lax.ppermute only.
A program may use at most 128 MiB of HBM per device.

```python
import math
import jax
import jax.numpy as jnp
import numpy as np
from jax import lax

D = 8192
FF = 28672
R = 64
RR = 4096
TOK_DEV = 56
EX_DEV = 4
TOKENS = 896
EXAMPLES = 64
QUERIES = 2048
N_DP = 16


def steps_of(own_key, dims, cuts, least, largest):
    def one(dim, shards_of):
        heights = jax.random.uniform(jax.random.fold_in(jax.random.fold_in(own_key, 6), dim), (shards_of,), jnp.float32, least / len(cuts), largest / len(cuts))
        return jnp.repeat(jnp.exp(heights), dims[dim] // shards_of).reshape((-1,) + (1,) * (len(dims) - dim - 1))

    level = one(*cuts[0])
    for cut in cuts[1:]:
        level = level * one(*cut)
    return level


def length_profile(number_of, total, bound, skew):
    portions = [(1 << 20) // math.isqrt(grade ** skew) + 1 for grade in range(2, number_of + 1)]
    rest, given = total - bound - (number_of - 1), [1] * (number_of - 1)
    while rest > 0:
        candidates = [i for i in range(number_of - 1) if given[i] < bound]
        pool, left = sum([portions[i] for i in candidates]), rest
        for i in candidates:
            extra = min(bound - given[i], max(1, left * portions[i] // pool), rest)
            given[i] = given[i] + extra
            rest = rest - extra
    return np.array([bound] + given)


def uneven_parts(stream_key, amount, total, most, lean):
    if amount == 2:
        one = jax.random.randint(stream_key, (), max(1, total - most), min(most, total - 1) + 1)
        return jnp.stack([one, total - one])
    sizes = jnp.asarray(length_profile(amount, total, most, lean), jnp.int32)
    pairs = (amount - 1) // 2
    giver, receiver = sizes[1:1 + 2 * pairs:2], sizes[2:2 + 2 * pairs:2]
    slack = jnp.minimum(giver - 1, most - receiver)
    passed = jax.random.randint(jax.random.fold_in(stream_key, 1), (pairs,), 0, 1 << 20) % (slack + 1)
    sizes = sizes.at[1:1 + 2 * pairs:2].set(giver - passed).at[2:2 + 2 * pairs:2].set(receiver + passed)
    return sizes[jax.random.permutation(jax.random.fold_in(stream_key, 2), amount)]


def normal_values(key, shape, spread, most, pieces=(), kind=jnp.bfloat16):
    result = spread * jax.random.normal(key, shape, jnp.float32)
    if pieces:
        result = result * steps_of(key, shape, pieces, -0.22, 0.18)
    return jnp.clip(result, -most, most).astype(kind)


def setup_inputs(seed: int = 0, part: int = 0) -> dict:
    key_list = jax.random.split(jax.random.key(seed), 9)
    own_keys = jax.random.split(jax.random.fold_in(key_list[8], part), 9)
    acts = normal_values(own_keys[0], (TOKENS, D), 1.0, 6.0, ((0, 16),))
    out_grad = normal_values(own_keys[1], (TOKENS, D), 1.0, 6.0, ((0, 16),))
    gate_factor = normal_values(own_keys[2], (TOKENS, FF), 0.5, 4.0, ((0, 16),))
    down_weight = normal_values(key_list[3], (FF, D), FF ** -0.5, 0.03125, ((0, 16),))
    proj_in = normal_values(key_list[4], (R, D), D ** -0.5, 0.0625)
    proj_out = normal_values(key_list[5], (R, FF), FF ** -0.5, 0.03125, ((1, 16),))
    lengths = jax.vmap(lambda own: uneven_parts(own, EX_DEV, TOK_DEV, TOK_DEV // 2, 2))(jax.random.split(own_keys[6], N_DP)).reshape((N_DP, EX_DEV)).astype(jnp.int32)
    queries = normal_values(key_list[7], (QUERIES, RR), 0.5, 4.0, ((0, 16),), jnp.float32)
    return {"acts": acts, "out_grad": out_grad, "gate_factor": gate_factor, "down_weight": down_weight, "proj_in": proj_in, "proj_out": proj_out, "lengths": lengths, "queries": queries}


def reference(acts, out_grad, gate_factor, down_weight, proj_in, proj_out, lengths, queries):
    width = FF // N_DP
    w_blocks = down_weight.reshape(N_DP, width, D)
    f_blocks = gate_factor.reshape(TOKENS, N_DP, width).transpose(1, 0, 2)
    p_blocks = proj_out.reshape(R, N_DP, width).transpose(1, 0, 2)

    def one_block(items):
        weight, factor, proj = items
        hidden = lax.dot_general(out_grad.astype(jnp.float32), weight.astype(jnp.float32), (((1,), (1,)), ((), ())), preferred_element_type=jnp.float32)
        hidden_grad = (hidden * factor.astype(jnp.float32)).astype(jnp.bfloat16)
        return lax.dot_general(hidden_grad.astype(jnp.float32), proj.astype(jnp.float32), (((1,), (1,)), ((), ())), preferred_element_type=jnp.float32)
    out_proj = jnp.sum(lax.map(one_block, (w_blocks, f_blocks, p_blocks)), axis=0)
    in_proj = lax.dot_general(acts.astype(jnp.float32), proj_in.astype(jnp.float32), (((1,), (1,)), ((), ())), preferred_element_type=jnp.float32)
    stop_at = jnp.cumsum(lengths, axis=1) + (jnp.arange(N_DP, dtype=jnp.int32) * TOK_DEV)[:, None]
    stop_at = stop_at.reshape(-1)
    starts = stop_at - lengths.reshape(-1)
    position = jnp.arange(TOKENS, dtype=jnp.int32)
    member = ((position[None, :] >= starts[:, None]) & (position[None, :] < stop_at[:, None])).astype(jnp.float32)
    outer_rows = (out_proj[:, :, None] * in_proj[:, None, :]).reshape(TOKENS, R * R)
    grads = jnp.dot(member, outer_rows, precision=lax.Precision.HIGHEST)
    gram = jnp.dot(grads, grads.T, precision=lax.Precision.HIGHEST)
    damping = 0.1 * jnp.trace(gram) / (EXAMPLES * EXAMPLES)
    system = gram / EXAMPLES + damping * jnp.eye(EXAMPLES, dtype=jnp.float32)
    against = jnp.dot(grads, queries.T, precision=lax.Precision.HIGHEST)
    factor = jnp.linalg.cholesky(system)
    return jax.scipy.linalg.cho_solve((factor, True), against)
```

```python
import functools

import jax
import jax.numpy as jnp
from jax import lax
from jax.experimental import pallas as pl
from jax.experimental.pallas import tpu as pltpu
from jax.sharding import PartitionSpec as P

AXIS = "dp"
HBM = pl.BlockSpec(memory_space=pl.ANY)
VMEM_LIMIT = 56 * 1024 * 1024


def contract_last(left, right):
    return lax.dot_general(
        left, right, (((1,), (1,)), ((), ())), preferred_element_type=jnp.float32
    )


def swap(block, bit, count):
    return lax.ppermute(block, AXIS, [(i, i ^ bit) for i in range(count)])


def line(block, pairs):
    return lax.ppermute(block, AXIS, [(4 * a + i, 4 * b + i) for a, b in pairs for i in range(4)])


def copies(pieces, shapes, *arrays):
    count = len(arrays)

    def body(*refs):
        ins, outs, sem = refs[:count], refs[count:-1], refs[-1]
        moves = pieces(lax.axis_index(AXIS), ins, outs)

        def each(act):
            for i, (when, src, dst) in enumerate(moves):
                move = pltpu.make_async_copy(src, dst, sem.at[i])
                if when is None:
                    act(move)
                else:
                    pl.when(when)(functools.partial(act, move))

        each(lambda move: move.start())
        each(lambda move: move.wait())

    total = sum(functools.reduce(lambda a, b: a * b, s) for s in shapes)
    return pl.pallas_call(
        body,
        out_shape=[jax.ShapeDtypeStruct(s, arrays[0].dtype) for s in shapes],
        in_specs=[HBM] * count,
        out_specs=[pl.BlockSpec(memory_space=pltpu.VMEM)] * len(shapes),
        scratch_shapes=[pltpu.SemaphoreType.DMA((32,))],
        cost_estimate=pl.CostEstimate(flops=0, bytes_accessed=total, transcendentals=0),
        name="copies",
    )(*arrays)


def either(first, second):
    def pieces(me, ins, outs):
        edge = (me < 4) | (me >= 12)
        lanes = first.shape[1] // 128
        number = next(n for n in (5, 4, 3, 2, 1) if lanes % n == 0)
        part = 128 * (lanes // number)
        cuts = [pl.ds(part * i, part) for i in range(number)]
        return [(edge, ins[0].at[:, cut], outs[0].at[:, cut]) for cut in cuts] + [
            (jnp.logical_not(edge), ins[1].at[:, cut], outs[0].at[:, cut]) for cut in cuts
        ]

    return copies(pieces, [first.shape], first, second)[0]


def fence(*arrays):
    def body(*refs):
        pass

    return pl.pallas_call(
        body,
        out_shape=[jax.ShapeDtypeStruct(a.shape, a.dtype) for a in arrays],
        in_specs=[HBM] * len(arrays),
        out_specs=[HBM] * len(arrays),
        input_output_aliases={i: i for i in range(len(arrays))},
        name="fence",
    )(*arrays)


def by_device(gate, count):
    rows, width = gate.shape[0], gate.shape[1] // count

    def pieces(me, ins, outs):
        return [(None, ins[0].at[:, pl.ds(i * width, width)], outs[0].at[i]) for i in range(count)]

    return copies(pieces, [(count, rows, width)], gate)[0]


def hidden_chunk(blocks, weight, tile=256):
    rows, wide = blocks[0].shape
    width, depth = weight.shape
    count = len(blocks)

    def body(*refs):
        ins, w, out, beside, stacked = refs[:count], *refs[count:]

        @pl.when(pl.program_id(0) == 0)
        def _():
            for i in range(count):
                stacked[64 * i : 64 * i + rows, :] = ins[i][:, :depth]
                beside[i, :rows] = ins[i][:, depth:].astype(jnp.float32)
                if rows < 64:
                    stacked[64 * i + rows : 64 * i + 64, :] = jnp.zeros((64 - rows, depth), stacked.dtype)
                    beside[i, rows:] = jnp.zeros((64 - rows, wide - depth), jnp.float32)

        out[...] = contract_last(stacked[...], w[...])

    return pl.pallas_call(
        body,
        grid=(width // tile,),
        out_shape=[
            jax.ShapeDtypeStruct((64 * count, width), jnp.float32),
            jax.ShapeDtypeStruct((count, 64, wide - depth), jnp.float32),
        ],
        in_specs=[pl.BlockSpec((rows, wide), lambda j: (0, 0), pipeline_mode=pl.Buffered(1))] * count
        + [pl.BlockSpec((tile, depth), lambda j: (j, 0))],
        out_specs=[
            pl.BlockSpec((64 * count, tile), lambda j: (0, j)),
            pl.BlockSpec((count, 64, wide - depth), lambda j: (0, 0, 0)),
        ],
        scratch_shapes=[pltpu.VMEM((64 * count, depth), jnp.bfloat16)],
        compiler_params=pltpu.CompilerParams(vmem_limit_bytes=VMEM_LIMIT),
        cost_estimate=pl.CostEstimate(flops=1, bytes_accessed=1, transcendentals=0),
        name="hidden_chunk",
    )(*blocks, weight)


def project(hiddens, gates, proj, lengths, tile=256):
    count, rows, width = gates.shape
    heads = proj.shape[0]
    slots = len(hiddens)

    def body(*refs):
        hs, g, p, spans, out, grads, total = refs[:slots], *refs[slots:]
        step = pl.program_id(0)
        me = lax.axis_index(AXIS)

        @pl.when(step == 0)
        def _():
            grads[...] = jnp.zeros_like(grads)
            total[...] = jnp.zeros_like(total)

        for m in range(slots):
            for r in range(4):
                gate = g[me ^ (4 * m + r)].astype(jnp.float32)
                at = 256 * m + 64 * r
                grads[at : at + rows, :] = (hs[m][64 * r : 64 * r + rows, :] * gate).astype(jnp.bfloat16)
        total[...] += contract_last(grads[...], p[...])

        @pl.when(step == pl.num_programs(0) - 1)
        def _():
            for r in range(4 * slots):
                block = total[64 * r : 64 * r + 64]
                if r == 0:
                    at = lax.broadcasted_iota(jnp.int32, block.shape, 0)
                    block = jnp.where(at == rows, spans[...], block)
                out[me ^ r] = jnp.concatenate([block[:32], block[32:]], axis=1)

    return pl.pallas_call(
        body,
        grid=(width // tile,),
        out_shape=jax.ShapeDtypeStruct((count, 32, 2 * heads), jnp.float32),
        in_specs=[pl.BlockSpec((256, tile), lambda j: (0, j))] * slots
        + [
            pl.BlockSpec((count, rows, tile), lambda j: (0, 0, j)),
            pl.BlockSpec((heads, tile), lambda j: (0, j)),
            pl.BlockSpec((1, heads), lambda j: (0, 0)),
        ],
        out_specs=pl.BlockSpec((count, 32, 2 * heads), lambda j: (0, 0, 0)),
        scratch_shapes=[pltpu.VMEM((256 * slots, tile), jnp.bfloat16), pltpu.VMEM((256 * slots, heads), jnp.float32)],
        compiler_params=pltpu.CompilerParams(vmem_limit_bytes=VMEM_LIMIT),
        cost_estimate=pl.CostEstimate(flops=1, bytes_accessed=1, transcendentals=0),
        name="project",
    )(*hiddens, gates, proj, lengths)


def partial_projection(rows, gate, weight, proj, lengths):
    pairs = [(0, 1), (1, 0), (2, 3), (3, 2)]
    middle = [(1, 2), (2, 1)]
    ends = [(1, 0), (2, 3)]

    def across(block):
        return swap(block, 2, 16)

    def core(block):
        return swap(block, 1, 16)

    near, mid, y0, c0 = line(rows, pairs), line(rows, middle), across(rows), core(rows)
    gates = by_device(gate, 16)
    near, mid, y0, c0, gates = fence(near, mid, y0, c0, gates)

    mid_far, out_mid, y1 = line(near, middle), line(mid, ends), across(near)
    c1, cy0 = core(near), core(y0)
    mid_far, out_mid, near, mid, y0, y1, c1, cy0, gates = fence(mid_far, out_mid, near, mid, y0, y1, c1, cy0, gates)

    gates = lax.all_to_all(gates, AXIS, split_axis=0, concat_axis=0, tiled=True)
    slot2 = either(out_mid, mid_far)
    out_far, y2 = line(mid_far, ends), across(slot2)
    c2, cy1 = core(slot2), core(y1)
    h0, i0 = hidden_chunk((rows, c0, y0, cy0), weight)
    out_far, mid, slot2, near, y1, c1, cy1, y2, c2, h0 = fence(out_far, mid, slot2, near, y1, c1, cy1, y2, c2, h0)

    slot3 = either(out_far, mid)
    y3 = across(slot3)
    c3, cy2 = core(slot3), core(y2)
    h1, i1 = hidden_chunk((near, c1, y1, cy1), weight)
    h2, i2 = hidden_chunk((slot2, c2, y2, cy2), weight)
    slot3, y3, c3, h1, h2 = fence(slot3, y3, c3, h1, h2)

    cy3 = core(y3)
    h3, i3 = hidden_chunk((slot3, c3, y3, cy3), weight)
    return project((h0, h1, h2, h3), gates, proj, lengths), jnp.concatenate([i0, i1, i2, i3], axis=0)


def eliminate(system, right):
    size = system.shape[0]
    at = lax.broadcasted_iota(jnp.int32, (size, 1), 0)
    for j in range(size):
        inverse = 1.0 / system[j : j + 1, j : j + 1]
        factor = jnp.where(at == j, 1.0 - inverse, system[:, j : j + 1] * inverse)
        system, right = system - factor * system[j : j + 1, :], right - factor * right[j : j + 1, :]
    return right


def finish(out_blocks, in_blocks, member, queries):
    count, _, heads = in_blocks.shape
    groups = count // 4
    examples = 4 * count
    wanted = queries.shape[0]
    exact = dict(precision=lax.Precision.HIGHEST, preferred_element_type=jnp.float32)

    def body(o, i, m, q, scores, left, double, both):
        both[:wanted, :] = q[...]
        double[...] = jnp.zeros_like(double)
        for g in range(groups):
            halves = [o[4 * g + r, :, part] for r in range(4) for part in (slice(heads), slice(heads, 2 * heads))]
            turned = jnp.concatenate(halves, axis=0).T
            inner = i[4 * g : 4 * g + 4].reshape(256, heads)
            double[:256, :heads] = inner
            double[256:, heads:] = inner
            mask = m[g]
            for p in range(heads // 2):
                left[16 * p : 16 * p + 16, :256] = mask * turned[2 * p : 2 * p + 1, :]
                left[16 * p : 16 * p + 16, 256:] = mask * turned[2 * p + 1 : 2 * p + 2, :]
            made = jnp.dot(left[...], double[...], **exact)
            for p in range(heads // 2):
                both[wanted + 16 * g : wanted + 16 * g + 16, 128 * p : 128 * p + 128] = made[16 * p : 16 * p + 16, :]
        grads = both[wanted:, :]
        products = lax.dot_general(grads, both[...], (((1,), (1,)), ((), ())), **exact)
        against, gram = products[:, :wanted], products[:, wanted:]
        row = lax.broadcasted_iota(jnp.int32, (examples, examples), 0)
        eye = (row == lax.broadcasted_iota(jnp.int32, (examples, examples), 1)).astype(jnp.float32)
        trace = jnp.sum(gram * eye, axis=(0, 1), keepdims=True)
        damping = 0.1 * trace / (examples * examples)
        scores[...] = eliminate(gram / examples + damping * eye, against)

    return pl.pallas_call(
        body,
        out_shape=jax.ShapeDtypeStruct((examples, wanted), jnp.float32),
        scratch_shapes=[
            pltpu.VMEM((8 * heads, 512), jnp.float32),
            pltpu.VMEM((512, 2 * heads), jnp.float32),
            pltpu.VMEM((wanted + examples, heads * heads), jnp.float32),
        ],
        compiler_params=pltpu.CompilerParams(vmem_limit_bytes=VMEM_LIMIT),
        name="finish",
    )(out_blocks, in_blocks, member, queries)


def reorder(blocks):
    return blocks[lax.axis_index(AXIS) ^ jnp.arange(blocks.shape[0])]


def in_place_order(beside, spans, rows):
    count = spans.shape[0]
    heads = beside.shape[2] // 2
    in_blocks = reorder(beside[:, :, :heads] + beside[:, :, heads:])
    stop_at = jnp.cumsum(spans, axis=1)
    position = jnp.arange(64, dtype=jnp.int32)
    inside = (position >= (stop_at - spans)[:, :, None]) & (position < stop_at[:, :, None])
    apart = jnp.eye(4, dtype=bool)[None, :, None, :, None] & inside.reshape(count // 4, 4, 4, 1, 64)
    return in_blocks, apart.astype(jnp.float32).reshape(count // 4, 16, 256)


def per_device(acts, out_grad, gate_factor, down_weight, proj_in, proj_out, lengths, queries):
    rows = acts.shape[0]
    count = gate_factor.shape[1] // down_weight.shape[0]
    heads = proj_in.shape[0]
    own = contract_last(acts, proj_in)
    high = lax.reduce_precision(own, 8, 7)
    low = (own - high).astype(jnp.bfloat16)
    sent = jnp.concatenate([out_grad, high.astype(jnp.bfloat16), low], axis=1)
    spans = jnp.pad(lengths.astype(jnp.float32), ((0, 0), (0, heads - 4)))
    if count == 16:
        partial, beside = partial_projection(sent, gate_factor, down_weight, proj_out, spans)
    else:
        sent = lax.all_gather(sent, AXIS, axis=0, tiled=True)
        factor = lax.all_to_all(gate_factor, AXIS, split_axis=1, concat_axis=0, tiled=True)
        hidden = contract_last(sent[:, : out_grad.shape[1]], down_weight)
        hidden_grad = (hidden * factor.astype(jnp.float32)).astype(jnp.bfloat16)
        partial = contract_last(hidden_grad, proj_out).reshape(count, rows, heads)
        partial = jnp.pad(partial, ((0, 0), (0, 64 - rows), (0, 0)))
        me = lax.axis_index(AXIS)
        partial = lax.dynamic_update_slice(partial, spans[None], (me, rows, 0))
        partial = jnp.concatenate([partial[:, :32], partial[:, 32:]], axis=2)
        beside = sent[:, out_grad.shape[1] :].astype(jnp.float32).reshape(count, rows, 2 * heads)
        beside = reorder(jnp.pad(beside, ((0, 0), (0, 64 - rows), (0, 0))))
    bit = 1
    while bit < count:
        partial = partial + swap(partial, bit, count)
        bit *= 2
    spans = partial[:, rows - 32, heads : heads + 4].astype(jnp.int32)
    in_blocks, member = in_place_order(beside, spans, rows)
    return finish(partial, in_blocks, member, queries)


def solution(mesh):
    return jax.shard_map(
        per_device,
        mesh=mesh,
        in_specs=(
            P(("groups", "dp"), None),
            P(("groups", "dp"), None),
            P(("groups", "dp"), None),
            P("dp", None),
            P(),
            P(None, "dp"),
            P(("groups", "dp"), None),
            P("dp", None),
        ),
        out_specs=P("groups", "dp"),
        check_vma=False,
    )
```

```python
import functools

import jax
import jax.numpy as jnp
from jax import lax
from jax.experimental import pallas as pl
from jax.experimental.pallas import tpu as pltpu
from jax.sharding import PartitionSpec as P

AXIS = "dp"
HBM = pl.BlockSpec(memory_space=pl.ANY)
VMEM_LIMIT = 56 * 1024 * 1024


def contract_last(left, right):
    return lax.dot_general(
        left, right, (((1,), (1,)), ((), ())), preferred_element_type=jnp.float32
    )


def swap(block, bit, count):
    return lax.ppermute(block, AXIS, [(i, i ^ bit) for i in range(count)])


def line(block, pairs):
    return lax.ppermute(block, AXIS, [(4 * a + i, 4 * b + i) for a, b in pairs for i in range(4)])


def fence(*arrays):
    def body(*refs):
        pass

    return pl.pallas_call(
        body,
        out_shape=[jax.ShapeDtypeStruct(a.shape, a.dtype) for a in arrays],
        in_specs=[HBM] * len(arrays),
        out_specs=[HBM] * len(arrays),
        input_output_aliases={i: i for i in range(len(arrays))},
        name="fence",
    )(*arrays)


def by_device(gate, inner, count, first):
    rows, width = gate.shape[0], gate.shape[1] // count
    lanes = inner.shape[1]

    def body(g, own, one, two, sem):
        moves = []
        for i in range(count):
            cuts = (
                (pl.ds(i * width, first), one.at[i, :, pl.ds(0, first)]),
                (pl.ds(i * width + first, width - first), two.at[i]),
            )
            for half, (src, dst) in enumerate(cuts):
                moves.append(pltpu.make_async_copy(g.at[:, src], dst, sem.at[half, i]))
        for move in moves:
            move.start()
        for i in range(count):
            one[i, :, first:] = own[...]
        for move in moves:
            move.wait()

    return pl.pallas_call(
        body,
        out_shape=[
            jax.ShapeDtypeStruct((count, rows, first + lanes), gate.dtype),
            jax.ShapeDtypeStruct((count, rows, width - first), gate.dtype),
        ],
        in_specs=[HBM, pl.BlockSpec(memory_space=pltpu.VMEM)],
        out_specs=[pl.BlockSpec(memory_space=pltpu.VMEM)] * 2,
        scratch_shapes=[pltpu.SemaphoreType.DMA((2, count))],
        compiler_params=pltpu.CompilerParams(vmem_limit_bytes=VMEM_LIMIT),
        cost_estimate=pl.CostEstimate(flops=1, bytes_accessed=1, transcendentals=0),
        name="by_device",
    )(gate, inner)


def hidden_chunk(blocks, weight, tile=256):
    rows, depth = blocks[0].shape
    width = weight.shape[0]
    count = len(blocks)

    def body(*refs):
        ins, w, out, stacked = refs[:count], *refs[count:]

        @pl.when(pl.program_id(0) == 0)
        def _():
            for i in range(count):
                stacked[64 * i : 64 * i + rows, :] = ins[i][...]
                if rows < 64:
                    stacked[64 * i + rows : 64 * i + 64, :] = jnp.zeros((64 - rows, depth), stacked.dtype)

        out[...] = contract_last(stacked[...], w[...])

    return pl.pallas_call(
        body,
        grid=(width // tile,),
        out_shape=jax.ShapeDtypeStruct((64 * count, width), jnp.float32),
        in_specs=[pl.BlockSpec((rows, depth), lambda j: (0, 0), pipeline_mode=pl.Buffered(1))] * count
        + [pl.BlockSpec((tile, depth), lambda j: (j, 0))],
        out_specs=pl.BlockSpec((64 * count, tile), lambda j: (0, j)),
        scratch_shapes=[pltpu.VMEM((64 * count, depth), jnp.bfloat16)],
        compiler_params=pltpu.CompilerParams(vmem_limit_bytes=VMEM_LIMIT),
        cost_estimate=pl.CostEstimate(flops=1, bytes_accessed=1, transcendentals=0),
        name="hidden_chunk",
    )(*blocks, weight)


def project(hiddens, gates, proj, start, columns, tile=256):
    count, rows, _ = gates.shape
    heads = proj.shape[0]
    slots = len(hiddens)
    skip = start // tile

    def body(*refs):
        hs, g, p, out, grads = refs[:slots], *refs[slots:]
        step = pl.program_id(0)
        me = lax.axis_index(AXIS)

        @pl.when(step == 0)
        def _():
            grads[...] = jnp.zeros_like(grads)
            out[...] = jnp.zeros_like(out)

        for m in range(slots):
            for r in range(4):
                gate = g[me ^ (4 * m + r)].astype(jnp.float32)
                at = 256 * m + 64 * r
                grads[at : at + rows, :] = (hs[m][64 * r : 64 * r + rows, :] * gate).astype(jnp.bfloat16)
        out[...] += contract_last(grads[...], p[...])

    return pl.pallas_call(
        body,
        grid=(columns // tile,),
        out_shape=jax.ShapeDtypeStruct((256 * slots, heads), jnp.float32),
        in_specs=[pl.BlockSpec((256, tile), lambda j: (0, j + skip))] * slots
        + [
            pl.BlockSpec((count, rows, tile), lambda j: (0, 0, j)),
            pl.BlockSpec((heads, tile), lambda j: (0, j + skip)),
        ],
        out_specs=pl.BlockSpec((256 * slots, heads), lambda j: (0, 0)),
        scratch_shapes=[pltpu.VMEM((256 * slots, tile), jnp.bfloat16)],
        compiler_params=pltpu.CompilerParams(vmem_limit_bytes=VMEM_LIMIT),
        cost_estimate=pl.CostEstimate(flops=1, bytes_accessed=1, transcendentals=0),
        name="project",
    )(*hiddens, gates, proj)


def arrange(one, two, lengths, rows):
    count, heads = one.shape[0] // 64, one.shape[1]

    def body(a, b, spans, kept, given):
        me = lax.axis_index(AXIS)
        even = me % 2 == 0
        for r in range(count):
            block = a[64 * r : 64 * r + 64, :] + b[64 * r : 64 * r + 64, :]
            if r == 0:
                at = lax.broadcasted_iota(jnp.int32, block.shape, 0)
                block = jnp.where(at == rows, spans[...], block)
            low = jnp.concatenate([block[:16], block[16:32]], axis=1)
            high = jnp.concatenate([block[32:48], block[48:]], axis=1)
            kept[me ^ r] = jnp.where(even, low, high)
            given[me ^ r] = jnp.where(even, high, low)

    return pl.pallas_call(
        body, out_shape=[jax.ShapeDtypeStruct((count, 16, 2 * heads), jnp.float32)] * 2, name="arrange"
    )(one, two, lengths)


def partial_projection(rows, gate, inner, weight, proj, lengths):
    first = weight.shape[0] * 3 // 7
    place = lax.axis_index(AXIS) // 4
    edge = (place == 0) | (place == 3)
    pairs = [(0, 1), (1, 0), (2, 3), (3, 2)]
    middle = [(1, 2), (2, 1)]
    ends = [(1, 0), (2, 3)]

    def across(block):
        return swap(block, 2, 16)

    def core(block):
        return swap(block, 1, 16)

    def exchange(block):
        return lax.all_to_all(block, AXIS, split_axis=0, concat_axis=0, tiled=True)

    near, mid, y0, c0 = line(rows, pairs), line(rows, middle), across(rows), core(rows)
    one, two = by_device(gate, inner, 16, first)
    near, mid, y0, c0, one, two = fence(near, mid, y0, c0, one, two)

    mid_far, out_mid, y1 = line(near, middle), line(mid, ends), across(near)
    c1, cy0 = core(near), core(y0)
    h0 = hidden_chunk((rows, c0, y0, cy0), weight)
    mid_far, out_mid, near, mid, y1, c1, h0, one, two = fence(mid_far, out_mid, near, mid, y1, c1, h0, one, two)

    slot2 = jnp.where(edge, out_mid, mid_far)
    out_far, y2 = line(mid_far, ends), across(slot2)
    c2, cy1 = core(slot2), core(y1)
    h1 = hidden_chunk((near, c1, y1, cy1), weight)
    h1, one = fence(h1, one)
    one = exchange(one)
    out_far, mid, slot2, y2, c2, two = fence(out_far, mid, slot2, y2, c2, two)

    slot3 = jnp.where(edge, out_far, mid)
    y3 = across(slot3)
    c3, cy2 = core(slot3), core(y2)
    h2 = hidden_chunk((slot2, c2, y2, cy2), weight)
    slot3, y3, c3, h2, one, two = fence(slot3, y3, c3, h2, one, two)

    cy3 = core(y3)
    two = exchange(two)
    h3 = hidden_chunk((slot3, c3, y3, cy3), weight)
    hiddens = (h0, h1, h2, h3)
    p1 = project(hiddens, one, proj, 0, first)
    p2 = project(hiddens, two, proj, first, weight.shape[0] - first)
    return arrange(p1, p2, lengths, rows.shape[0]), one[:, :, first:]


def eliminate(system, right):
    size = system.shape[0]
    both = jnp.concatenate([system, right], axis=1)
    at = lax.broadcasted_iota(jnp.int32, (size, 1), 0)
    for j in range(0, size, 2):
        one, two = (jnp.broadcast_to(both[:, j + k : j + k + 1], both.shape) for k in range(2))
        a, b, c, d = one[j : j + 1], two[j : j + 1], one[j + 1 : j + 2], two[j + 1 : j + 2]
        inverse = 1.0 / (a * d - b * c)
        first, second = both[j : j + 1], both[j + 1 : j + 2]
        first, second = (d * first - b * second) * inverse, (a * second - c * first) * inverse
        both = both - jnp.where(at == j, a - 1.0, one) * first - jnp.where(at == j + 1, d - 1.0, two) * second
    return both[:, size:]


def halves(block):
    high = block.astype(jnp.bfloat16)
    return high, (block - high.astype(jnp.float32)).astype(jnp.bfloat16)


def product(left, right, dims):
    def one(a, b):
        return lax.dot_general(a, b, (dims, ((), ())), preferred_element_type=jnp.float32)

    return one(left[0], right[0]) + (one(left[0], right[1]) + one(left[1], right[0]))


def finish(kept, given, in_blocks, member, queries):
    count, _, heads = in_blocks.shape
    groups = count // 4
    examples = 4 * count
    wanted = queries.shape[0]

    def body(own, other, i, m, q, scores, left, double, grads):
        even = lax.axis_index(AXIS) % 2 == 0
        double[...] = jnp.zeros_like(double)
        for g in range(groups):
            parts = []
            for r in range(4):
                low = jnp.where(even, own[4 * g + r], other[4 * g + r])
                high = jnp.where(even, other[4 * g + r], own[4 * g + r])
                parts += [low[:, :heads], low[:, heads:], high[:, :heads], high[:, heads:]]
            turned = jnp.concatenate(parts, axis=0).T
            inner = i[4 * g : 4 * g + 4].reshape(256, heads)
            double[:256, :heads] = inner
            double[256:, heads:] = inner
            mask = m[g]
            for p in range(heads // 2):
                left[16 * p : 16 * p + 16, :256] = mask * turned[2 * p : 2 * p + 1, :]
                left[16 * p : 16 * p + 16, 256:] = mask * turned[2 * p + 1 : 2 * p + 2, :]
            made = product(halves(left[...]), halves(double[...]), ((1,), (0,)))
            for p in range(heads // 2):
                grads[16 * g : 16 * g + 16, 128 * p : 128 * p + 128] = made[16 * p : 16 * p + 16, :]
        made = halves(grads[...])
        last = ((1,), (1,))
        against = product(halves(q[...]), made, last).T
        gram = product(made, made, last)
        row = lax.broadcasted_iota(jnp.int32, (examples, examples), 0)
        eye = (row == lax.broadcasted_iota(jnp.int32, (examples, examples), 1)).astype(jnp.float32)
        trace = jnp.sum(gram * eye, axis=(0, 1), keepdims=True)
        damping = 0.1 * trace / (examples * examples)
        scores[...] = eliminate(gram / examples + damping * eye, against)

    return pl.pallas_call(
        body,
        out_shape=jax.ShapeDtypeStruct((examples, wanted), jnp.float32),
        scratch_shapes=[
            pltpu.VMEM((8 * heads, 512), jnp.float32),
            pltpu.VMEM((512, 2 * heads), jnp.float32),
            pltpu.VMEM((examples, heads * heads), jnp.float32),
        ],
        compiler_params=pltpu.CompilerParams(vmem_limit_bytes=VMEM_LIMIT),
        name="finish",
    )(kept, given, in_blocks, member, queries)


def in_place_order(inner, spans, rows):
    count = spans.shape[0]
    heads = inner.shape[2] // 2
    inner = jnp.pad(inner.astype(jnp.float32), ((0, 0), (0, 64 - rows), (0, 0)))
    in_blocks = inner[:, :, :heads] + inner[:, :, heads:]
    stop_at = jnp.cumsum(spans, axis=1)
    position = jnp.arange(64, dtype=jnp.int32)
    inside = (position >= (stop_at - spans)[:, :, None]) & (position < stop_at[:, :, None])
    apart = jnp.eye(4, dtype=bool)[None, :, None, :, None] & inside.reshape(count // 4, 4, 4, 1, 64)
    return in_blocks, apart.astype(jnp.float32).reshape(count // 4, 16, 256)


def per_device(acts, out_grad, gate_factor, down_weight, proj_in, proj_out, lengths, queries):
    rows = acts.shape[0]
    count = gate_factor.shape[1] // down_weight.shape[0]
    heads = proj_in.shape[0]
    own = contract_last(acts, proj_in)
    high = lax.reduce_precision(own, 8, 7)
    low = (own - high).astype(jnp.bfloat16)
    inner = jnp.concatenate([high.astype(jnp.bfloat16), low], axis=1)
    spans = jnp.pad(lengths.astype(jnp.float32), ((0, 0), (0, heads - 4)))
    if count == 16:
        (kept, given), inner = partial_projection(out_grad, gate_factor, inner, down_weight, proj_out, spans)
    else:
        inner = lax.all_gather(inner, AXIS)
        factor = lax.all_to_all(gate_factor, AXIS, split_axis=1, concat_axis=0, tiled=True)
        hidden = contract_last(lax.all_gather(out_grad, AXIS, axis=0, tiled=True), down_weight)
        hidden_grad = (hidden * factor.astype(jnp.float32)).astype(jnp.bfloat16)
        partial = contract_last(hidden_grad, proj_out).reshape(count, rows, heads)
        partial = jnp.pad(partial, ((0, 0), (0, 64 - rows), (0, 0)))
        partial = lax.dynamic_update_slice(partial, spans[None], (lax.axis_index(AXIS), rows, 0))
        low, high = (jnp.concatenate([half[:, :16], half[:, 16:]], axis=2) for half in (partial[:, :32], partial[:, 32:]))
        even = lax.axis_index(AXIS) % 2 == 0
        kept, given = jnp.where(even, low, high), jnp.where(even, high, low)
    kept = kept + swap(given, 1, count)
    bit = 2
    while bit < count:
        kept = kept + swap(kept, bit, count)
        bit *= 2
    given = swap(kept, 1, count)
    high = jnp.where(lax.axis_index(AXIS) % 2 == 0, given, kept)
    at = rows - 32
    spans = high[:, at % 16, heads * (at // 16) : heads * (at // 16) + 4].astype(jnp.int32)
    in_blocks, member = in_place_order(inner, spans, rows)
    return finish(kept, given, in_blocks, member, queries)


def solution(mesh):
    return jax.shard_map(
        per_device,
        mesh=mesh,
        in_specs=(
            P(("groups", "dp"), None),
            P(("groups", "dp"), None),
            P(("groups", "dp"), None),
            P("dp", None),
            P(),
            P(None, "dp"),
            P(("groups", "dp"), None),
            P("dp", None),
        ),
        out_specs=P("groups", "dp"),
        check_vma=False,
    )
```

```python
import functools

import jax
import jax.numpy as jnp
from jax import lax
from jax.experimental import pallas as pl
from jax.experimental.pallas import tpu as pltpu
from jax.sharding import PartitionSpec as P

AXIS = "dp"
HBM = pl.BlockSpec(memory_space=pl.ANY)
VMEM_LIMIT = 56 * 1024 * 1024


def contract_last(left, right):
    return lax.dot_general(
        left, right, (((1,), (1,)), ((), ())), preferred_element_type=jnp.float32
    )


def swap(block, bit, count):
    return lax.ppermute(block, AXIS, [(i, i ^ bit) for i in range(count)])


def line(block, pairs):
    return lax.ppermute(block, AXIS, [(4 * a + i, 4 * b + i) for a, b in pairs for i in range(4)])


def fence(*arrays):
    def body(*refs):
        pass

    return pl.pallas_call(
        body,
        out_shape=[jax.ShapeDtypeStruct(a.shape, a.dtype) for a in arrays],
        in_specs=[HBM] * len(arrays),
        out_specs=[HBM] * len(arrays),
        input_output_aliases={i: i for i in range(len(arrays))},
        name="fence",
    )(*arrays)


def by_device(gate, inner, count, parts):
    rows, width = gate.shape[0], gate.shape[1] // count
    lanes = inner.shape[1]

    def body(g, own, *refs):
        outs, sem = refs[:-1], refs[-1]
        moves = []
        for i in range(count):
            start = i * width
            for k, size in enumerate(parts):
                src, dst = g.at[:, pl.ds(start, size)], outs[k].at[i, :, pl.ds(0, size)]
                moves.append(pltpu.make_async_copy(src, dst, sem.at[k, i]))
                start += size
        for move in moves:
            move.start()
        for i in range(count):
            outs[0][i, :, parts[0] :] = own[...]
        for move in moves:
            move.wait()

    sizes = [parts[0] + lanes, *parts[1:]]
    return pl.pallas_call(
        body,
        out_shape=[jax.ShapeDtypeStruct((count, rows, size), gate.dtype) for size in sizes],
        in_specs=[HBM, pl.BlockSpec(memory_space=pltpu.VMEM)],
        out_specs=[pl.BlockSpec(memory_space=pltpu.VMEM)] * len(parts),
        scratch_shapes=[pltpu.SemaphoreType.DMA((len(parts), count))],
        compiler_params=pltpu.CompilerParams(vmem_limit_bytes=VMEM_LIMIT),
        cost_estimate=pl.CostEstimate(flops=1, bytes_accessed=1, transcendentals=0),
        name="by_device",
    )(gate, inner)


def hidden_chunk(blocks, weight, tile=256):
    rows, depth = blocks[0].shape
    width = weight.shape[0]
    count = len(blocks)

    def body(*refs):
        ins, w, out, stacked = refs[:count], *refs[count:]

        @pl.when(pl.program_id(0) == 0)
        def _():
            for i in range(count):
                stacked[64 * i : 64 * i + rows, :] = ins[i][...]
                if rows < 64:
                    stacked[64 * i + rows : 64 * i + 64, :] = jnp.zeros((64 - rows, depth), stacked.dtype)

        out[...] = contract_last(stacked[...], w[...])

    return pl.pallas_call(
        body,
        grid=(width // tile,),
        out_shape=jax.ShapeDtypeStruct((64 * count, width), jnp.float32),
        in_specs=[pl.BlockSpec((rows, depth), lambda j: (0, 0), pipeline_mode=pl.Buffered(1))] * count
        + [pl.BlockSpec((tile, depth), lambda j: (j, 0))],
        out_specs=pl.BlockSpec((64 * count, tile), lambda j: (0, j)),
        scratch_shapes=[pltpu.VMEM((64 * count, depth), jnp.bfloat16)],
        compiler_params=pltpu.CompilerParams(vmem_limit_bytes=VMEM_LIMIT),
        cost_estimate=pl.CostEstimate(flops=1, bytes_accessed=1, transcendentals=0),
        name="hidden_chunk",
    )(*blocks, weight)


def project(hiddens, gates, proj, start, columns, before=None, lengths=None, tile=256):
    count, rows, _ = gates.shape
    heads = proj.shape[0]
    slots = len(hiddens)
    skip = start // tile
    more = [a for a in (before, lengths) if a is not None]

    def body(*refs):
        hs, g, p = refs[:slots], refs[slots], refs[slots + 1]
        total, grads = refs[-2:]
        outs = refs[slots + 2 + len(more) : -2]
        step = pl.program_id(0)
        me = lax.axis_index(AXIS)

        @pl.when(step == 0)
        def _():
            grads[...] = jnp.zeros_like(grads)
            total[...] = jnp.zeros_like(total) if before is None else refs[slots + 2][...]

        for m in range(slots):
            for r in range(4):
                gate = g[me ^ (4 * m + r)].astype(jnp.float32)
                at = 256 * m + 64 * r
                grads[at : at + rows, :] = (hs[m][64 * r : 64 * r + rows, :] * gate).astype(jnp.bfloat16)
        total[...] += contract_last(grads[...], p[...])

        @pl.when(step == pl.num_programs(0) - 1)
        def _():
            if lengths is None:
                outs[0][...] = total[...]
                return
            even = me % 2 == 0
            for r in range(4 * slots):
                block = total[64 * r : 64 * r + 64]
                if r == 0:
                    at = lax.broadcasted_iota(jnp.int32, block.shape, 0)
                    block = jnp.where(at == rows, refs[slots + 3][...], block)
                low = jnp.concatenate([block[:16], block[16:32]], axis=1)
                high = jnp.concatenate([block[32:48], block[48:]], axis=1)
                outs[0][me ^ r] = jnp.where(even, low, high)
                outs[1][me ^ r] = jnp.where(even, high, low)

    if lengths is None:
        shapes = [(256 * slots, heads)]
    else:
        shapes = [(count, 16, 2 * heads)] * 2
    outs = pl.pallas_call(
        body,
        grid=(columns // tile,),
        out_shape=[jax.ShapeDtypeStruct(shape, jnp.float32) for shape in shapes],
        in_specs=[pl.BlockSpec((256, tile), lambda j: (0, j + skip))] * slots
        + [
            pl.BlockSpec((count, rows, tile), lambda j: (0, 0, j)),
            pl.BlockSpec((heads, tile), lambda j: (0, j + skip)),
        ]
        + [pl.BlockSpec(a.shape, lambda j: (0, 0)) for a in more],
        out_specs=[pl.BlockSpec(shape, lambda j, rank=len(shape): (0,) * rank) for shape in shapes],
        scratch_shapes=[
            pltpu.VMEM((256 * slots, heads), jnp.float32),
            pltpu.VMEM((256 * slots, tile), jnp.bfloat16),
        ],
        compiler_params=pltpu.CompilerParams(vmem_limit_bytes=VMEM_LIMIT),
        cost_estimate=pl.CostEstimate(flops=1, bytes_accessed=1, transcendentals=0),
        name="project",
    )(*hiddens, gates, proj, *more)
    return outs[0] if lengths is None else outs


def partial_projection(rows, gate, inner, weight, proj, lengths):
    parts = [weight.shape[0] // 7 * k for k in (3,4)]
    place = lax.axis_index(AXIS) // 4
    edge = (place == 0) | (place == 3)
    pairs = [(0, 1), (1, 0), (2, 3), (3, 2)]
    middle = [(1, 2), (2, 1)]
    ends = [(1, 0), (2, 3)]

    def across(block):
        return swap(block, 2, 16)

    def core(block):
        return swap(block, 1, 16)

    def exchange(block):
        return lax.all_to_all(block, AXIS, split_axis=0, concat_axis=0, tiled=True)

    near, mid, y0, c0 = line(rows, pairs), line(rows, middle), across(rows), core(rows)
    g0, g1 = by_device(gate, inner, 16, parts)
    near, mid, y0, c0, g0, g1 = fence(near, mid, y0, c0, g0, g1)

    mid_far, out_mid, y1 = line(near, middle), line(mid, ends), across(near)
    c1, cy0 = core(near), core(y0)
    h0 = hidden_chunk((rows, c0, y0, cy0), weight)
    mid_far, out_mid, near, mid, y1, c1, h0, g0, g1 = fence(mid_far, out_mid, near, mid, y1, c1, h0, g0, g1)

    slot2 = jnp.where(edge, out_mid, mid_far)
    out_far, y2 = line(mid_far, ends), across(slot2)
    c2, cy1 = core(slot2), core(y1)
    h1 = hidden_chunk((near, c1, y1, cy1), weight)
    h1, g0 = fence(h1, g0)
    g0 = exchange(g0)
    out_far, mid, slot2, y2, c2, g1 = fence(out_far, mid, slot2, y2, c2, g1)

    slot3 = jnp.where(edge, out_far, mid)
    y3 = across(slot3)
    c3, cy2 = core(slot3), core(y2)
    h2 = hidden_chunk((slot2, c2, y2, cy2), weight)
    slot3, y3, c3, h2, g0, g1 = fence(slot3, y3, c3, h2, g0, g1)

    cy3 = core(y3)
    g1 = exchange(g1)
    h3 = hidden_chunk((slot3, c3, y3, cy3), weight)
    hiddens = (h0, h1, h2, h3)
    sums, start = None, 0
    for k, gates in enumerate((g0, g1)):
        sums = project(hiddens, gates, proj, start, parts[k], sums, lengths if k == len(parts) - 1 else None)
        start += parts[k]
    return sums, g0[:, :, parts[0] :]


def eliminate(system, right):
    size = system.shape[0]
    both = jnp.concatenate([system, right], axis=1)
    at = lax.broadcasted_iota(jnp.int32, (size, 1), 0)
    for j in range(0, size, 2):
        one, two = (jnp.broadcast_to(both[:, j + k : j + k + 1], both.shape) for k in range(2))
        a, b, c, d = one[j : j + 1], two[j : j + 1], one[j + 1 : j + 2], two[j + 1 : j + 2]
        inverse = 1.0 / (a * d - b * c)
        first, second = both[j : j + 1], both[j + 1 : j + 2]
        first, second = (d * first - b * second) * inverse, (a * second - c * first) * inverse
        both = both - jnp.where(at == j, a - 1.0, one) * first - jnp.where(at == j + 1, d - 1.0, two) * second
    return both[:, size:]


def halves(block):
    high = block.astype(jnp.bfloat16)
    return high, (block - high.astype(jnp.float32)).astype(jnp.bfloat16)


def product(left, right, dims):
    def one(a, b):
        return lax.dot_general(a, b, (dims, ((), ())), preferred_element_type=jnp.float32)

    return one(left[0], right[0]) + (one(left[0], right[1]) + one(left[1], right[0]))


def places(spans):
    row = lax.broadcasted_iota(jnp.int32, (16, 256), 0)
    start = stop = jnp.zeros((16, 256), jnp.float32)
    for r, span in enumerate(spans):
        end = jnp.zeros((1, 1), jnp.float32)
        for j in range(4):
            start = jnp.where(row == 4 * r + j, end, start)
            end = end + span[:, j : j + 1]
            stop = jnp.where(row == 4 * r + j, end, stop)
    at = (lax.broadcasted_iota(jnp.int32, (16, 256), 1) - 64 * (row // 4)).astype(jnp.float32)
    return jnp.where((at >= start) & (at < stop), 1.0, 0.0)


def finish(kept, given, in_blocks, queries, rows):
    count, _, heads = in_blocks.shape
    groups = count // 4
    examples = 4 * count
    wanted = queries.shape[0]

    at = rows - 32

    def body(own, other, i, q, scores, left, double, grads):
        even = lax.axis_index(AXIS) % 2 == 0
        double[...] = jnp.zeros_like(double)
        for g in range(groups):
            parts, spans = [], []
            for r in range(4):
                low = jnp.where(even, own[4 * g + r], other[4 * g + r])
                high = jnp.where(even, other[4 * g + r], own[4 * g + r])
                parts += [low[:, :heads], low[:, heads:], high[:, :heads], high[:, heads:]]
                spans.append(high[at % 16 : at % 16 + 1, heads * (at // 16) : heads * (at // 16) + 4])
            turned = jnp.concatenate(parts, axis=0).T
            inner = i[4 * g : 4 * g + 4].reshape(256, heads)
            double[:256, :heads] = inner
            double[256:, heads:] = inner
            mask = places(spans)
            for p in range(heads // 2):
                left[16 * p : 16 * p + 16, :256] = mask * turned[2 * p : 2 * p + 1, :]
                left[16 * p : 16 * p + 16, 256:] = mask * turned[2 * p + 1 : 2 * p + 2, :]
            made = product(halves(left[...]), halves(double[...]), ((1,), (0,)))
            for p in range(heads // 2):
                grads[16 * g : 16 * g + 16, 128 * p : 128 * p + 128] = made[16 * p : 16 * p + 16, :]
        made = halves(grads[...])
        last = ((1,), (1,))
        against = product(halves(q[...]), made, last).T
        gram = product(made, made, last)
        row = lax.broadcasted_iota(jnp.int32, (examples, examples), 0)
        eye = (row == lax.broadcasted_iota(jnp.int32, (examples, examples), 1)).astype(jnp.float32)
        trace = jnp.sum(gram * eye, axis=(0, 1), keepdims=True)
        damping = 0.1 * trace / (examples * examples)
        scores[...] = eliminate(gram / examples + damping * eye, against)

    return pl.pallas_call(
        body,
        out_shape=jax.ShapeDtypeStruct((examples, wanted), jnp.float32),
        scratch_shapes=[
            pltpu.VMEM((8 * heads, 512), jnp.float32),
            pltpu.VMEM((512, 2 * heads), jnp.float32),
            pltpu.VMEM((examples, heads * heads), jnp.float32),
        ],
        compiler_params=pltpu.CompilerParams(vmem_limit_bytes=24 * 1024 * 1024),
        name="finish",
    )(kept, given, in_blocks, queries)


def per_device(acts, out_grad, gate_factor, down_weight, proj_in, proj_out, lengths, queries):
    rows = acts.shape[0]
    count = gate_factor.shape[1] // down_weight.shape[0]
    heads = proj_in.shape[0]
    own = contract_last(acts, proj_in)
    high = lax.reduce_precision(own, 8, 7)
    low = (own - high).astype(jnp.bfloat16)
    inner = jnp.concatenate([high.astype(jnp.bfloat16), low], axis=1)
    spans = jnp.pad(lengths.astype(jnp.float32), ((0, 0), (0, heads - 4)))
    if count == 16:
        (kept, given), inner = partial_projection(out_grad, gate_factor, inner, down_weight, proj_out, spans)
    else:
        inner = lax.all_gather(inner, AXIS)
        factor = lax.all_to_all(gate_factor, AXIS, split_axis=1, concat_axis=0, tiled=True)
        hidden = contract_last(lax.all_gather(out_grad, AXIS, axis=0, tiled=True), down_weight)
        hidden_grad = (hidden * factor.astype(jnp.float32)).astype(jnp.bfloat16)
        partial = contract_last(hidden_grad, proj_out).reshape(count, rows, heads)
        partial = jnp.pad(partial, ((0, 0), (0, 64 - rows), (0, 0)))
        partial = lax.dynamic_update_slice(partial, spans[None], (lax.axis_index(AXIS), rows, 0))
        low, high = (jnp.concatenate([half[:, :16], half[:, 16:]], axis=2) for half in (partial[:, :32], partial[:, 32:]))
        even = lax.axis_index(AXIS) % 2 == 0
        kept, given = jnp.where(even, low, high), jnp.where(even, high, low)
    kept = kept + swap(given, 1, count)
    bit = 2
    while bit < count:
        kept = kept + swap(kept, bit, count)
        bit *= 2
    given = swap(kept, 1, count)
    inner = jnp.pad(inner.astype(jnp.float32), ((0, 0), (0, 64 - rows), (0, 0)))
    return finish(kept, given, inner[:, :, :heads] + inner[:, :, heads:], queries, rows)


def solution(mesh):
    return jax.shard_map(
        per_device,
        mesh=mesh,
        in_specs=(
            P(("groups", "dp"), None),
            P(("groups", "dp"), None),
            P(("groups", "dp"), None),
            P("dp", None),
            P(),
            P(None, "dp"),
            P(("groups", "dp"), None),
            P("dp", None),
        ),
        out_specs=P("groups", "dp"),
        check_vma=False,
    )
```

```python
import functools

import jax
import jax.numpy as jnp
from jax import lax
from jax.experimental import pallas as pl
from jax.experimental.pallas import tpu as pltpu
from jax.sharding import PartitionSpec as P

AXIS = "dp"
HBM = pl.BlockSpec(memory_space=pl.ANY)
VMEM_LIMIT = 56 * 1024 * 1024


def contract_last(left, right):
    return lax.dot_general(
        left, right, (((1,), (1,)), ((), ())), preferred_element_type=jnp.float32
    )


def swap(block, bit, count):
    return lax.ppermute(block, AXIS, [(i, i ^ bit) for i in range(count)])


def line(block, pairs):
    return lax.ppermute(block, AXIS, [(4 * a + i, 4 * b + i) for a, b in pairs for i in range(4)])


def fence(*arrays):
    def body(*refs):
        pass

    return pl.pallas_call(
        body,
        out_shape=[jax.ShapeDtypeStruct(a.shape, a.dtype) for a in arrays],
        in_specs=[HBM] * len(arrays),
        out_specs=[HBM] * len(arrays),
        input_output_aliases={i: i for i in range(len(arrays))},
        name="fence",
    )(*arrays)


def by_device(gate, inner, count, parts):
    rows, width = gate.shape[0], gate.shape[1] // count
    lanes = inner.shape[1]

    def body(g, own, *refs):
        outs, sem = refs[:-1], refs[-1]
        moves = []
        for i in range(count):
            start = i * width
            for k, size in enumerate(parts):
                src, dst = g.at[:, pl.ds(start, size)], outs[k].at[i, :, pl.ds(0, size)]
                moves.append(pltpu.make_async_copy(src, dst, sem.at[k, i]))
                start += size
        for move in moves:
            move.start()
        for i in range(count):
            outs[0][i, :, parts[0] :] = own[...]
        for move in moves:
            move.wait()

    sizes = [parts[0] + lanes, *parts[1:]]
    return pl.pallas_call(
        body,
        out_shape=[jax.ShapeDtypeStruct((count, rows, size), gate.dtype) for size in sizes],
        in_specs=[HBM, pl.BlockSpec(memory_space=pltpu.VMEM)],
        out_specs=[pl.BlockSpec(memory_space=pltpu.VMEM)] * len(parts),
        scratch_shapes=[pltpu.SemaphoreType.DMA((len(parts), count))],
        compiler_params=pltpu.CompilerParams(vmem_limit_bytes=VMEM_LIMIT),
        cost_estimate=pl.CostEstimate(flops=1, bytes_accessed=1, transcendentals=0),
        name="by_device",
    )(gate, inner)


def hidden_chunk(blocks, weight, tile=256):
    rows, depth = blocks[0].shape
    width = weight.shape[0]
    count = len(blocks)

    def body(*refs):
        ins, w, out, stacked = refs[:count], *refs[count:]

        @pl.when(pl.program_id(0) == 0)
        def _():
            for i in range(count):
                stacked[64 * i : 64 * i + rows, :] = ins[i][...]
                if rows < 64:
                    stacked[64 * i + rows : 64 * i + 64, :] = jnp.zeros((64 - rows, depth), stacked.dtype)

        out[...] = contract_last(stacked[...], w[...])

    return pl.pallas_call(
        body,
        grid=(width // tile,),
        out_shape=jax.ShapeDtypeStruct((64 * count, width), jnp.float32),
        in_specs=[pl.BlockSpec((rows, depth), lambda j: (0, 0), pipeline_mode=pl.Buffered(1))] * count
        + [pl.BlockSpec((tile, depth), lambda j: (j, 0))],
        out_specs=pl.BlockSpec((64 * count, tile), lambda j: (0, j)),
        scratch_shapes=[pltpu.VMEM((64 * count, depth), jnp.bfloat16)],
        compiler_params=pltpu.CompilerParams(vmem_limit_bytes=VMEM_LIMIT),
        cost_estimate=pl.CostEstimate(flops=1, bytes_accessed=1, transcendentals=0),
        name="hidden_chunk",
    )(*blocks, weight)


def project(hiddens, gates, proj, start, columns, before=None, lengths=None, tile=256):
    count, rows, _ = gates.shape
    heads = proj.shape[0]
    slots = len(hiddens)
    skip = start // tile
    more = [a for a in (before, lengths) if a is not None]

    def body(*refs):
        hs, g, p = refs[:slots], refs[slots], refs[slots + 1]
        total, grads = refs[-2:]
        outs = refs[slots + 2 + len(more) : -2]
        step = pl.program_id(0)
        me = lax.axis_index(AXIS)

        @pl.when(step == 0)
        def _():
            grads[...] = jnp.zeros_like(grads)
            total[...] = jnp.zeros_like(total) if before is None else refs[slots + 2][...]

        for m in range(slots):
            for r in range(4):
                gate = g[me ^ (4 * m + r)].astype(jnp.float32)
                at = 256 * m + 64 * r
                grads[at : at + rows, :] = (hs[m][64 * r : 64 * r + rows, :] * gate).astype(jnp.bfloat16)
        total[...] += contract_last(grads[...], p[...])

        @pl.when(step == pl.num_programs(0) - 1)
        def _():
            if lengths is None:
                outs[0][...] = total[...]
                return
            even = me % 2 == 0
            for r in range(4 * slots):
                block = total[64 * r : 64 * r + 64]
                if r == 0:
                    at = lax.broadcasted_iota(jnp.int32, block.shape, 0)
                    block = jnp.where(at == rows, refs[slots + 3][...], block)
                low = jnp.concatenate([block[:16], block[16:32]], axis=1)
                high = jnp.concatenate([block[32:48], block[48:]], axis=1)
                outs[0][me ^ r] = jnp.where(even, low, high)
                outs[1][me ^ r] = jnp.where(even, high, low)

    if lengths is None:
        shapes = [(256 * slots, heads)]
    else:
        shapes = [(count, 16, 2 * heads)] * 2
    outs = pl.pallas_call(
        body,
        grid=(columns // tile,),
        out_shape=[jax.ShapeDtypeStruct(shape, jnp.float32) for shape in shapes],
        in_specs=[pl.BlockSpec((256, tile), lambda j: (0, j + skip))] * slots
        + [
            pl.BlockSpec((count, rows, tile), lambda j: (0, 0, j)),
            pl.BlockSpec((heads, tile), lambda j: (0, j + skip)),
        ]
        + [pl.BlockSpec(a.shape, lambda j: (0, 0)) for a in more],
        out_specs=[pl.BlockSpec(shape, lambda j, rank=len(shape): (0,) * rank) for shape in shapes],
        scratch_shapes=[
            pltpu.VMEM((256 * slots, heads), jnp.float32),
            pltpu.VMEM((256 * slots, tile), jnp.bfloat16),
        ],
        compiler_params=pltpu.CompilerParams(vmem_limit_bytes=VMEM_LIMIT),
        cost_estimate=pl.CostEstimate(flops=1, bytes_accessed=1, transcendentals=0),
        name="project",
    )(*hiddens, gates, proj, *more)
    return outs[0] if lengths is None else outs


def partial_projection(rows, gate, inner, weight, proj, lengths):
    parts = [weight.shape[0] // 7 * k for k in (3,4)]
    place = lax.axis_index(AXIS) // 4
    edge = (place == 0) | (place == 3)
    pairs = [(0, 1), (1, 0), (2, 3), (3, 2)]
    middle = [(1, 2), (2, 1)]

    def across(block):
        return swap(block, 2, 16)

    def core(block):
        return swap(block, 1, 16)

    def exchange(block):
        return lax.all_to_all(block, AXIS, split_axis=0, concat_axis=0, tiled=True)

    near, mid, y0, c0 = line(rows, pairs), line(rows, middle), across(rows), core(rows)
    g0, g1 = by_device(gate, inner, 16, parts)
    near, mid, y0, c0, g0, g1 = fence(near, mid, y0, c0, g0, g1)

    mid_far, out_mid, y1 = line(near, middle), line(mid, pairs), across(near)
    c1, cy0 = core(near), core(y0)
    h0 = hidden_chunk((rows, c0, y0, cy0), weight)
    mid_far, out_mid, near, mid, y1, c1, h0, g0, g1 = fence(mid_far, out_mid, near, mid, y1, c1, h0, g0, g1)

    slot2 = jnp.where(edge, out_mid, mid_far)
    out_far, y2 = line(mid_far, pairs), across(slot2)
    c2, cy1 = core(slot2), core(y1)
    h1 = hidden_chunk((near, c1, y1, cy1), weight)
    h1, g0 = fence(h1, g0)
    g0 = exchange(g0)
    out_far, mid, slot2, y2, c2, g1 = fence(out_far, mid, slot2, y2, c2, g1)

    slot3 = jnp.where(edge, out_far, mid)
    y3 = across(slot3)
    c3, cy2 = core(slot3), core(y2)
    h2 = hidden_chunk((slot2, c2, y2, cy2), weight)
    slot3, y3, c3, h2, g0, g1 = fence(slot3, y3, c3, h2, g0, g1)

    cy3 = core(y3)
    g1 = exchange(g1)
    h3 = hidden_chunk((slot3, c3, y3, cy3), weight)
    hiddens = (h0, h1, h2, h3)
    sums, start = None, 0
    for k, gates in enumerate((g0, g1)):
        sums = project(hiddens, gates, proj, start, parts[k], sums, lengths if k == len(parts) - 1 else None)
        start += parts[k]
    return sums, g0[:, :, parts[0] :]


def eliminate(system, right):
    size = system.shape[0]
    both = jnp.concatenate([system, right], axis=1)
    at = lax.broadcasted_iota(jnp.int32, (size, 1), 0)
    for j in range(0, size, 2):
        one, two = (jnp.broadcast_to(both[:, j + k : j + k + 1], both.shape) for k in range(2))
        a, b, c, d = one[j : j + 1], two[j : j + 1], one[j + 1 : j + 2], two[j + 1 : j + 2]
        inverse = 1.0 / (a * d - b * c)
        first, second = both[j : j + 1], both[j + 1 : j + 2]
        first, second = (d * first - b * second) * inverse, (a * second - c * first) * inverse
        both = both - jnp.where(at == j, a - 1.0, one) * first - jnp.where(at == j + 1, d - 1.0, two) * second
    return both[:, size:]


def halves(block):
    high = block.astype(jnp.bfloat16)
    return high, (block - high.astype(jnp.float32)).astype(jnp.bfloat16)


def product(left, right, dims):
    def one(a, b):
        return lax.dot_general(a, b, (dims, ((), ())), preferred_element_type=jnp.float32)

    return one(left[0], right[0]) + (one(left[0], right[1]) + one(left[1], right[0]))


def places(spans):
    row = lax.broadcasted_iota(jnp.int32, (16, 256), 0)
    start = stop = jnp.zeros((16, 256), jnp.float32)
    for r, span in enumerate(spans):
        end = jnp.zeros((1, 1), jnp.float32)
        for j in range(4):
            start = jnp.where(row == 4 * r + j, end, start)
            end = end + span[:, j : j + 1]
            stop = jnp.where(row == 4 * r + j, end, stop)
    at = (lax.broadcasted_iota(jnp.int32, (16, 256), 1) - 64 * (row // 4)).astype(jnp.float32)
    return jnp.where((at >= start) & (at < stop), 1.0, 0.0)


def finish(kept, given, in_blocks, queries, rows):
    count, _, heads = in_blocks.shape
    groups = count // 4
    examples = 4 * count
    wanted = queries.shape[0]

    at = rows - 32

    def body(own, other, i, q, scores, left, double, grads):
        even = lax.axis_index(AXIS) % 2 == 0
        double[...] = jnp.zeros_like(double)
        for g in range(groups):
            parts, spans = [], []
            for r in range(4):
                low = jnp.where(even, own[4 * g + r], other[4 * g + r])
                high = jnp.where(even, other[4 * g + r], own[4 * g + r])
                parts += [low[:, :heads], low[:, heads:], high[:, :heads], high[:, heads:]]
                spans.append(high[at % 16 : at % 16 + 1, heads * (at // 16) : heads * (at // 16) + 4])
            turned = jnp.concatenate(parts, axis=0).T
            inner = i[4 * g : 4 * g + 4].reshape(256, heads)
            double[:256, :heads] = inner
            double[256:, heads:] = inner
            mask = places(spans)
            for p in range(heads // 2):
                left[16 * p : 16 * p + 16, :256] = mask * turned[2 * p : 2 * p + 1, :]
                left[16 * p : 16 * p + 16, 256:] = mask * turned[2 * p + 1 : 2 * p + 2, :]
            made = product(halves(left[...]), halves(double[...]), ((1,), (0,)))
            for p in range(heads // 2):
                grads[16 * g : 16 * g + 16, 128 * p : 128 * p + 128] = made[16 * p : 16 * p + 16, :]
        made = halves(grads[...])
        last = ((1,), (1,))
        against = product(halves(q[...]), made, last).T
        gram = product(made, made, last)
        row = lax.broadcasted_iota(jnp.int32, (examples, examples), 0)
        eye = (row == lax.broadcasted_iota(jnp.int32, (examples, examples), 1)).astype(jnp.float32)
        trace = jnp.sum(gram * eye, axis=(0, 1), keepdims=True)
        damping = 0.1 * trace / (examples * examples)
        scores[...] = eliminate(gram / examples + damping * eye, against)

    return pl.pallas_call(
        body,
        out_shape=jax.ShapeDtypeStruct((examples, wanted), jnp.float32),
        scratch_shapes=[
            pltpu.VMEM((8 * heads, 512), jnp.float32),
            pltpu.VMEM((512, 2 * heads), jnp.float32),
            pltpu.VMEM((examples, heads * heads), jnp.float32),
        ],
        compiler_params=pltpu.CompilerParams(vmem_limit_bytes=24 * 1024 * 1024),
        name="finish",
    )(kept, given, in_blocks, queries)


def per_device(acts, out_grad, gate_factor, down_weight, proj_in, proj_out, lengths, queries):
    rows = acts.shape[0]
    count = gate_factor.shape[1] // down_weight.shape[0]
    heads = proj_in.shape[0]
    own = contract_last(acts, proj_in)
    high = lax.reduce_precision(own, 8, 7)
    low = (own - high).astype(jnp.bfloat16)
    inner = jnp.concatenate([high.astype(jnp.bfloat16), low], axis=1)
    spans = jnp.pad(lengths.astype(jnp.float32), ((0, 0), (0, heads - 4)))
    if count == 16:
        (kept, given), inner = partial_projection(out_grad, gate_factor, inner, down_weight, proj_out, spans)
    else:
        inner = lax.all_gather(inner, AXIS)
        factor = lax.all_to_all(gate_factor, AXIS, split_axis=1, concat_axis=0, tiled=True)
        hidden = contract_last(lax.all_gather(out_grad, AXIS, axis=0, tiled=True), down_weight)
        hidden_grad = (hidden * factor.astype(jnp.float32)).astype(jnp.bfloat16)
        partial = contract_last(hidden_grad, proj_out).reshape(count, rows, heads)
        partial = jnp.pad(partial, ((0, 0), (0, 64 - rows), (0, 0)))
        partial = lax.dynamic_update_slice(partial, spans[None], (lax.axis_index(AXIS), rows, 0))
        low, high = (jnp.concatenate([half[:, :16], half[:, 16:]], axis=2) for half in (partial[:, :32], partial[:, 32:]))
        even = lax.axis_index(AXIS) % 2 == 0
        kept, given = jnp.where(even, low, high), jnp.where(even, high, low)
    kept = kept + swap(given, 1, count)
    bit = 2
    while bit < count:
        kept = kept + swap(kept, bit, count)
        bit *= 2
    given = swap(kept, 1, count)
    inner = jnp.pad(inner.astype(jnp.float32), ((0, 0), (0, 64 - rows), (0, 0)))
    return finish(kept, given, inner[:, :, :heads] + inner[:, :, heads:], queries, rows)


def solution(mesh):
    return jax.shard_map(
        per_device,
        mesh=mesh,
        in_specs=(
            P(("groups", "dp"), None),
            P(("groups", "dp"), None),
            P(("groups", "dp"), None),
            P("dp", None),
            P(),
            P(None, "dp"),
            P(("groups", "dp"), None),
            P("dp", None),
        ),
        out_specs=P("groups", "dp"),
        check_vma=False,
    )
```

```python
import functools

import jax
import jax.numpy as jnp
from jax import lax
from jax.experimental import pallas as pl
from jax.experimental.pallas import tpu as pltpu
from jax.sharding import PartitionSpec as P

AXIS = "dp"
HBM = pl.BlockSpec(memory_space=pl.ANY)
VMEM_LIMIT = 56 * 1024 * 1024


def contract_last(left, right):
    return lax.dot_general(
        left, right, (((1,), (1,)), ((), ())), preferred_element_type=jnp.float32
    )


def swap(block, bit, count):
    return lax.ppermute(block, AXIS, [(i, i ^ bit) for i in range(count)])


def line(block, pairs):
    return lax.ppermute(block, AXIS, [(4 * a + i, 4 * b + i) for a, b in pairs for i in range(4)])


def fence(*arrays):
    def body(*refs):
        pass

    return pl.pallas_call(
        body,
        out_shape=[jax.ShapeDtypeStruct(a.shape, a.dtype) for a in arrays],
        in_specs=[HBM] * len(arrays),
        out_specs=[HBM] * len(arrays),
        input_output_aliases={i: i for i in range(len(arrays))},
        name="fence",
    )(*arrays)


def by_device(gate, inner, count, parts):
    rows, width = gate.shape[0], gate.shape[1] // count
    lanes = inner.shape[1]

    def body(g, own, *refs):
        outs, sem = refs[:-1], refs[-1]
        moves = []
        for i in range(count):
            start = i * width
            for k, size in enumerate(parts):
                src, dst = g.at[:, pl.ds(start, size)], outs[k].at[i, :, pl.ds(0, size)]
                moves.append(pltpu.make_async_copy(src, dst, sem.at[k, i]))
                start += size
        for move in moves:
            move.start()
        for i in range(count):
            outs[0][i, :, parts[0] :] = own[...]
        for move in moves:
            move.wait()

    sizes = [parts[0] + lanes, *parts[1:]]
    return pl.pallas_call(
        body,
        out_shape=[jax.ShapeDtypeStruct((count, rows, size), gate.dtype) for size in sizes],
        in_specs=[HBM, pl.BlockSpec(memory_space=pltpu.VMEM)],
        out_specs=[pl.BlockSpec(memory_space=pltpu.VMEM)] * len(parts),
        scratch_shapes=[pltpu.SemaphoreType.DMA((len(parts), count))],
        compiler_params=pltpu.CompilerParams(vmem_limit_bytes=VMEM_LIMIT),
        cost_estimate=pl.CostEstimate(flops=1, bytes_accessed=1, transcendentals=0),
        name="by_device",
    )(gate, inner)


def hidden_chunk(blocks, weight, start=0, columns=None, tile=256):
    rows, depth = blocks[0].shape
    width = columns or weight.shape[0]
    skip = start // tile
    count = len(blocks)

    def body(*refs):
        ins, w, out, stacked = refs[:count], *refs[count:]

        @pl.when(pl.program_id(0) == 0)
        def _():
            for i in range(count):
                stacked[64 * i : 64 * i + rows, :] = ins[i][...]
                if rows < 64:
                    stacked[64 * i + rows : 64 * i + 64, :] = jnp.zeros((64 - rows, depth), stacked.dtype)

        out[...] = contract_last(stacked[...], w[...])

    return pl.pallas_call(
        body,
        grid=(width // tile,),
        out_shape=jax.ShapeDtypeStruct((64 * count, width), jnp.float32),
        in_specs=[pl.BlockSpec((rows, depth), lambda j: (0, 0), pipeline_mode=pl.Buffered(1))] * count
        + [pl.BlockSpec((tile, depth), lambda j: (j + skip, 0))],
        out_specs=pl.BlockSpec((64 * count, tile), lambda j: (0, j)),
        scratch_shapes=[pltpu.VMEM((64 * count, depth), jnp.bfloat16)],
        compiler_params=pltpu.CompilerParams(vmem_limit_bytes=VMEM_LIMIT),
        cost_estimate=pl.CostEstimate(flops=1, bytes_accessed=1, transcendentals=0),
        name="hidden_chunk",
    )(*blocks, weight)


def project(hiddens, gates, proj, start, columns, before=None, lengths=None, tile=256):
    count, rows, _ = gates.shape
    heads = proj.shape[0]
    slots = len(hiddens)
    skip = start // tile
    more = [a for a in (before, lengths) if a is not None]

    def body(*refs):
        hs, g, p = refs[:slots], refs[slots], refs[slots + 1]
        total, grads = refs[-2:]
        outs = refs[slots + 2 + len(more) : -2]
        step = pl.program_id(0)
        me = lax.axis_index(AXIS)

        @pl.when(step == 0)
        def _():
            grads[...] = jnp.zeros_like(grads)
            total[...] = jnp.zeros_like(total) if before is None else refs[slots + 2][...]

        for m in range(slots):
            for r in range(4):
                gate = g[me ^ (4 * m + r)].astype(jnp.float32)
                at = 256 * m + 64 * r
                grads[at : at + rows, :] = (hs[m][64 * r : 64 * r + rows, :] * gate).astype(jnp.bfloat16)
        total[...] += contract_last(grads[...], p[...])

        @pl.when(step == pl.num_programs(0) - 1)
        def _():
            if lengths is None:
                outs[0][...] = total[...]
                return
            even = me % 2 == 0
            for r in range(4 * slots):
                block = total[64 * r : 64 * r + 64]
                if r == 0:
                    at = lax.broadcasted_iota(jnp.int32, block.shape, 0)
                    block = jnp.where(at == rows, refs[slots + 3][...], block)
                low = jnp.concatenate([block[:16], block[16:32]], axis=1)
                high = jnp.concatenate([block[32:48], block[48:]], axis=1)
                outs[0][me ^ r] = jnp.where(even, low, high)
                outs[1][me ^ r] = jnp.where(even, high, low)

    if lengths is None:
        shapes = [(256 * slots, heads)]
    else:
        shapes = [(count, 16, 2 * heads)] * 2
    outs = pl.pallas_call(
        body,
        grid=(columns // tile,),
        out_shape=[jax.ShapeDtypeStruct(shape, jnp.float32) for shape in shapes],
        in_specs=[
            pl.BlockSpec((256, tile), lambda j, at=skip if h.shape[1] > columns else 0: (0, j + at)) for h in hiddens
        ]
        + [
            pl.BlockSpec((count, rows, tile), lambda j: (0, 0, j)),
            pl.BlockSpec((heads, tile), lambda j: (0, j + skip)),
        ]
        + [pl.BlockSpec(a.shape, lambda j: (0, 0)) for a in more],
        out_specs=[pl.BlockSpec(shape, lambda j, rank=len(shape): (0,) * rank) for shape in shapes],
        scratch_shapes=[
            pltpu.VMEM((256 * slots, heads), jnp.float32),
            pltpu.VMEM((256 * slots, tile), jnp.bfloat16),
        ],
        compiler_params=pltpu.CompilerParams(vmem_limit_bytes=VMEM_LIMIT),
        cost_estimate=pl.CostEstimate(flops=1, bytes_accessed=1, transcendentals=0),
        name="project",
    )(*hiddens, gates, proj, *more)
    return outs[0] if lengths is None else outs


def partial_projection(rows, gate, inner, weight, proj, lengths):
    parts = [weight.shape[0] // 7 * k for k in (3,4)]
    place = lax.axis_index(AXIS) // 4
    edge = (place == 0) | (place == 3)
    pairs = [(0, 1), (1, 0), (2, 3), (3, 2)]
    middle = [(1, 2), (2, 1)]

    def across(block):
        return swap(block, 2, 16)

    def core(block):
        return swap(block, 1, 16)

    def exchange(block):
        return lax.all_to_all(block, AXIS, split_axis=0, concat_axis=0, tiled=True)

    near, mid, y0, c0 = line(rows, pairs), line(rows, middle), across(rows), core(rows)
    g0, g1 = by_device(gate, inner, 16, parts)
    near, mid, y0, c0, g0, g1 = fence(near, mid, y0, c0, g0, g1)

    mid_far, out_mid, y1 = line(near, middle), line(mid, pairs), across(near)
    c1, cy0 = core(near), core(y0)
    h0 = hidden_chunk((rows, c0, y0, cy0), weight)
    mid_far, out_mid, near, mid, y1, c1, h0, g0, g1 = fence(mid_far, out_mid, near, mid, y1, c1, h0, g0, g1)

    slot2 = jnp.where(edge, out_mid, mid_far)
    out_far, y2 = line(mid_far, pairs), across(slot2)
    c2, cy1 = core(slot2), core(y1)
    h1 = [hidden_chunk((near, c1, y1, cy1), weight, 0, parts[0])]
    h1[0], y1, g0 = fence(h1[0], y1, g0)
    g0 = exchange(g0)
    h1.append(hidden_chunk((near, c1, y1, cy1), weight, parts[0], parts[1]))
    out_far, mid, slot2, y2, c2, h1[1], g1 = fence(out_far, mid, slot2, y2, c2, h1[1], g1)

    slot3 = jnp.where(edge, out_far, mid)
    y3 = across(slot3)
    c3, cy2 = core(slot3), core(y2)
    h2 = hidden_chunk((slot2, c2, y2, cy2), weight)
    slot3, y3, c3, h2, g1 = fence(slot3, y3, c3, h2, g1)

    cy3 = core(y3)
    g1 = exchange(g1)
    h3 = hidden_chunk((slot3, c3, y3, cy3), weight)
    sums, start = None, 0
    for k, gates in enumerate((g0, g1)):
        sums = project((h0, h1[k], h2, h3), gates, proj, start, parts[k], sums, lengths if k == len(parts) - 1 else None)
        start += parts[k]
    return sums, g0[:, :, parts[0] :]


def eliminate(system, right):
    size = system.shape[0]
    both = jnp.concatenate([system, right], axis=1)
    at = lax.broadcasted_iota(jnp.int32, (size, 1), 0)
    for j in range(0, size, 2):
        one, two = (jnp.broadcast_to(both[:, j + k : j + k + 1], both.shape) for k in range(2))
        a, b, c, d = one[j : j + 1], two[j : j + 1], one[j + 1 : j + 2], two[j + 1 : j + 2]
        inverse = 1.0 / (a * d - b * c)
        first, second = both[j : j + 1], both[j + 1 : j + 2]
        first, second = (d * first - b * second) * inverse, (a * second - c * first) * inverse
        both = both - jnp.where(at == j, a - 1.0, one) * first - jnp.where(at == j + 1, d - 1.0, two) * second
    return both[:, size:]


def halves(block):
    high = block.astype(jnp.bfloat16)
    return high, (block - high.astype(jnp.float32)).astype(jnp.bfloat16)


def product(left, right, dims):
    def one(a, b):
        return lax.dot_general(a, b, (dims, ((), ())), preferred_element_type=jnp.float32)

    return one(left[0], right[0]) + (one(left[0], right[1]) + one(left[1], right[0]))


def places(spans):
    row = lax.broadcasted_iota(jnp.int32, (16, 256), 0)
    start = stop = jnp.zeros((16, 256), jnp.float32)
    for r, span in enumerate(spans):
        end = jnp.zeros((1, 1), jnp.float32)
        for j in range(4):
            start = jnp.where(row == 4 * r + j, end, start)
            end = end + span[:, j : j + 1]
            stop = jnp.where(row == 4 * r + j, end, stop)
    at = (lax.broadcasted_iota(jnp.int32, (16, 256), 1) - 64 * (row // 4)).astype(jnp.float32)
    return jnp.where((at >= start) & (at < stop), 1.0, 0.0)


def finish(kept, given, in_blocks, queries, rows):
    count, _, heads = in_blocks.shape
    groups = count // 4
    examples = 4 * count
    wanted = queries.shape[0]

    at = rows - 32

    def body(own, other, i, q, scores, left, double, grads):
        even = lax.axis_index(AXIS) % 2 == 0
        double[...] = jnp.zeros_like(double)
        for g in range(groups):
            parts, spans = [], []
            for r in range(4):
                low = jnp.where(even, own[4 * g + r], other[4 * g + r])
                high = jnp.where(even, other[4 * g + r], own[4 * g + r])
                parts += [low[:, :heads], low[:, heads:], high[:, :heads], high[:, heads:]]
                spans.append(high[at % 16 : at % 16 + 1, heads * (at // 16) : heads * (at // 16) + 4])
            turned = jnp.concatenate(parts, axis=0).T
            inner = i[4 * g : 4 * g + 4].reshape(256, heads)
            double[:256, :heads] = inner
            double[256:, heads:] = inner
            mask = places(spans)
            for p in range(heads // 2):
                left[16 * p : 16 * p + 16, :256] = mask * turned[2 * p : 2 * p + 1, :]
                left[16 * p : 16 * p + 16, 256:] = mask * turned[2 * p + 1 : 2 * p + 2, :]
            made = product(halves(left[...]), halves(double[...]), ((1,), (0,)))
            for p in range(heads // 2):
                grads[16 * g : 16 * g + 16, 128 * p : 128 * p + 128] = made[16 * p : 16 * p + 16, :]
        made = halves(grads[...])
        last = ((1,), (1,))
        against = product(halves(q[...]), made, last).T
        gram = product(made, made, last)
        row = lax.broadcasted_iota(jnp.int32, (examples, examples), 0)
        eye = (row == lax.broadcasted_iota(jnp.int32, (examples, examples), 1)).astype(jnp.float32)
        trace = jnp.sum(gram * eye, axis=(0, 1), keepdims=True)
        damping = 0.1 * trace / (examples * examples)
        scores[...] = eliminate(gram / examples + damping * eye, against)

    return pl.pallas_call(
        body,
        out_shape=jax.ShapeDtypeStruct((examples, wanted), jnp.float32),
        scratch_shapes=[
            pltpu.VMEM((8 * heads, 512), jnp.float32),
            pltpu.VMEM((512, 2 * heads), jnp.float32),
            pltpu.VMEM((examples, heads * heads), jnp.float32),
        ],
        compiler_params=pltpu.CompilerParams(vmem_limit_bytes=24 * 1024 * 1024),
        name="finish",
    )(kept, given, in_blocks, queries)


def per_device(acts, out_grad, gate_factor, down_weight, proj_in, proj_out, lengths, queries):
    rows = acts.shape[0]
    count = gate_factor.shape[1] // down_weight.shape[0]
    heads = proj_in.shape[0]
    own = contract_last(acts, proj_in)
    high = lax.reduce_precision(own, 8, 7)
    low = (own - high).astype(jnp.bfloat16)
    inner = jnp.concatenate([high.astype(jnp.bfloat16), low], axis=1)
    spans = jnp.pad(lengths.astype(jnp.float32), ((0, 0), (0, heads - 4)))
    if count == 16:
        (kept, given), inner = partial_projection(out_grad, gate_factor, inner, down_weight, proj_out, spans)
    else:
        inner = lax.all_gather(inner, AXIS)
        factor = lax.all_to_all(gate_factor, AXIS, split_axis=1, concat_axis=0, tiled=True)
        hidden = contract_last(lax.all_gather(out_grad, AXIS, axis=0, tiled=True), down_weight)
        hidden_grad = (hidden * factor.astype(jnp.float32)).astype(jnp.bfloat16)
        partial = contract_last(hidden_grad, proj_out).reshape(count, rows, heads)
        partial = jnp.pad(partial, ((0, 0), (0, 64 - rows), (0, 0)))
        partial = lax.dynamic_update_slice(partial, spans[None], (lax.axis_index(AXIS), rows, 0))
        low, high = (jnp.concatenate([half[:, :16], half[:, 16:]], axis=2) for half in (partial[:, :32], partial[:, 32:]))
        even = lax.axis_index(AXIS) % 2 == 0
        kept, given = jnp.where(even, low, high), jnp.where(even, high, low)
    kept = kept + swap(given, 1, count)
    bit = 2
    while bit < count:
        kept = kept + swap(kept, bit, count)
        bit *= 2
    given = swap(kept, 1, count)
    inner = jnp.pad(inner.astype(jnp.float32), ((0, 0), (0, 64 - rows), (0, 0)))
    return finish(kept, given, inner[:, :, :heads] + inner[:, :, heads:], queries, rows)


def solution(mesh):
    return jax.shard_map(
        per_device,
        mesh=mesh,
        in_specs=(
            P(("groups", "dp"), None),
            P(("groups", "dp"), None),
            P(("groups", "dp"), None),
            P("dp", None),
            P(),
            P(None, "dp"),
            P(("groups", "dp"), None),
            P("dp", None),
        ),
        out_specs=P("groups", "dp"),
        check_vma=False,
    )
```
